32 devices in a mesh: work: 4 (over x, core), serv: 8 (over z, y).
Axes of the slice: x: 2, y: 2, z: 4, core: 2. Of those that a mesh axis runs over, the one named last changes fastest.
Arguments:
- user_factors: float32 [12288, 512], P(('work', 'serv')), may hold values from -6 to 6
- ratings: bfloat16 [12288, 8192], P(('work', 'serv')), may hold values from -6 to 6
- row_mask: int32 [12288, 16], P(('work', 'serv')), may hold values 0 or 1
- touched: int32 [32, 16], P(('work', 'serv')), may hold values from 0 to 31, as said below
- stale_cache: bfloat16 [262144, 512], P(('work', 'serv')), may hold values from -0.25 to 0.25
- item_factors: float32 [16384, 512], P('serv'), may hold values from -0.25 to 0.25
- roster: int32 [4], P('work'), may hold values from 0 to 7
Outputs:
- users_next: float32 [12288, 512], P(('work', 'serv'))
- items_next: float32 [16384, 512], P('serv')
The draws below stay inside these ranges and needn't reach their ends.
Inputs may be any that keep to these rules, and one draw needn't show every extreme that they name: `touched`: each row holds 16 different blocks; a block's server is its number // 4; each server named in a row is named by exactly 2 of its entries, so 8 servers a row; every row of worker d = w * 8 + j names server roster[w].
All inputs are finite; a program needn't handle non-finite values. No bound on the sum of `row_mask` on one device may be relied on, other than what follows from the above.
Results may differ from the reference program's by a relative error of at most 0.004.
Values may be sent and summed in bfloat16 or wider, within the bound.
A program may use at most 256 MiB of HBM per device.

```python
import jax
import jax.numpy as jnp
from jax import lax

R = 512
B = 512
UD = 384
BPS = 4
CAP = 2
OWN = 8
K = 16
NB_ALL = 32
WORKERS = 32
USERS = 12288
N_WORK = 4
N_SERV = 8


def shared_roster(key):
    key_base, key_pos = jax.random.split(jax.random.fold_in(key, 23), 2)
    base = jax.random.randint(key_base, (N_WORK,), 0, N_SERV)
    first = jax.random.randint(key_pos, (), 0, N_WORK)
    second = (first + 1) % N_WORK
    slots = jnp.arange(N_WORK, dtype=jnp.int32)
    base = jnp.where(slots == first, 0, base)
    base = jnp.where(slots == second, N_SERV - 1, base)
    return base.astype(jnp.int32)


def draw_roster(key, part):
    return shared_roster(key)


def draw_touched(key, part):
    key_pop, key_score, key_pick = jax.random.split(jax.random.fold_in(key, 17), 3)
    plan = shared_roster(key)
    hot_rows = jnp.repeat(plan, N_SERV)
    popular = jax.random.randint(key_pop, (N_SERV,), 0, 3)
    servers = jnp.arange(N_SERV, dtype=jnp.int32)
    scores = jax.random.randint(key_score, (WORKERS, N_SERV), 0, 1024) + popular[None, :] * 1024
    scores = scores * N_SERV + servers[None, :]
    scores = jnp.where(servers[None, :] == hot_rows[:, None], 100000000, scores)
    _, owners = lax.top_k(scores, OWN)
    ranks = jax.random.randint(key_pick, (WORKERS, OWN, BPS), 0, 1024) * BPS + jnp.arange(BPS, dtype=jnp.int32)
    picks = jnp.argsort(ranks, axis=-1)[:, :, :CAP]
    ids = owners[:, :, None] * BPS + picks
    return ids.reshape(WORKERS, OWN * CAP).astype(jnp.int32)


def set_ends(result, key, low, top_value):
    longest = result.shape.index(max(result.shape))
    spots = []
    for shift in (0, 1):
        where = [jax.random.randint(jax.random.fold_in(key, axis), (), 0, length) for axis, length in enumerate(result.shape)]
        where[longest] = (where[longest] + shift) % result.shape[longest]
        spots.append(tuple(where))
    return result.at[spots[0]].set(low).at[spots[1]].set(top_value)


def block_scale(rng, shape, cuts, smallest, high):
    gain = 1.0
    for axis_at, blocks in cuts:
        draws = jax.random.uniform(jax.random.fold_in(jax.random.fold_in(rng, 6), axis_at), (blocks,), jnp.float32, smallest / len(cuts), high / len(cuts))
        gain = gain * jnp.repeat(jnp.exp(draws), shape[axis_at] // blocks).reshape((-1,) + (1,) * (len(shape) - 1 - axis_at))
    return gain


def gaussian(key, dims, spread, bound, pieces=(), kind=jnp.bfloat16):
    drawn = jax.random.normal(key, dims, jnp.float32) * spread
    if len(pieces) > 0:
        drawn = block_scale(key, dims, pieces, -0.22, 0.18) * drawn
    return jnp.clip(drawn, min=-bound, max=bound).astype(kind)


def setup_inputs(seed: int = 0) -> dict:
    seeds = jax.random.split(jax.random.key(seed), 8)
    user_factors = gaussian(seeds[0], (USERS, R), 1.0, 6.0, ((0, 32),), jnp.float32)
    ratings = gaussian(seeds[1], (USERS, K * B), 1.0, 6.0, ((0, 32),))
    row_mask = set_ends((jax.random.randint(seeds[2], (USERS, K), 0, 4) < 3).astype(jnp.int32), jax.random.fold_in(seeds[2], 1), 0, 1)
    touched = draw_touched(jax.random.fold_in(seeds[7], 71), 0)
    stale_cache = gaussian(seeds[4], (WORKERS * K * B, R), R ** -0.5, 0.25, ((0, 32),))
    item_factors = gaussian(seeds[5], (NB_ALL * B, R), R ** -0.5, 0.25, ((0, 8),), jnp.float32)
    roster = draw_roster(jax.random.fold_in(seeds[7], 71), 0)
    return dict(user_factors=user_factors, ratings=ratings, row_mask=row_mask, touched=touched, stale_cache=stale_cache, item_factors=item_factors, roster=roster)


def reference(user_factors, ratings, row_mask, touched, stale_cache, item_factors, roster):
    fresh = item_factors.astype(jnp.bfloat16).reshape(NB_ALL, B, R)
    stale = stale_cache.reshape(WORKERS, K, B, R)

    def step(carry, dev):
        ids = touched[dev]
        owner_now = roster[dev // N_SERV]
        used = jnp.where((ids // BPS == owner_now)[:, None, None], fresh[ids], stale[dev]).astype(jnp.float32)
        start = (dev * UD).astype(jnp.int32)
        rows = lax.dynamic_slice_in_dim(user_factors, start, UD, 0)
        user_b = rows.astype(jnp.bfloat16).astype(jnp.float32)
        rate = lax.dynamic_slice_in_dim(ratings, start, UD, 0).astype(jnp.float32).reshape(UD, K, B)
        marks = lax.dynamic_slice_in_dim(row_mask, start, UD, 0).astype(jnp.float32)
        pred = jnp.einsum('ur,kbr->ukb', user_b, used)
        err = (marks[:, :, None] * (rate - pred)).astype(jnp.bfloat16).astype(jnp.float32)
        item_grad = jnp.einsum('ukb,ur->kbr', err, user_b)
        user_grad = jnp.einsum('ukb,kbr->ur', err, used)
        new_rows = rows - 0.05 * (0.1 * rows - user_grad)
        return carry.at[ids].add(item_grad), new_rows

    init = jnp.zeros((NB_ALL, B, R), jnp.float32)
    grad_sum, new_users = lax.scan(step, init, jnp.arange(WORKERS, dtype=jnp.int32))
    users_next = new_users.reshape(USERS, R)
    items_next = item_factors - 0.01 * (grad_sum.reshape(NB_ALL * B, R) + 0.1 * item_factors)
    return (users_next, items_next)
```

```python
import functools

import jax
import jax.numpy as jnp
from jax import lax
from jax.experimental import pallas as pl
from jax.experimental.pallas import tpu as pltpu
from jax.sharding import PartitionSpec as P

BPS = 4
CAP = 2
CHUNKS = 2
GROUPS = ((8, "wsz"), (8, "swz"))


def tile_kernel(rows, tile_ref, fresh_ref, pick_ref, core_ref, user_ref, mark_ref, rate_ref, stale_ref, new_ref,
                keep_ref, send_ref, ugrad_ref, grad_ref):
    slot = pl.program_id(0)

    @pl.when(slot == 0)
    def _():
        ugrad_ref[...] = jnp.zeros_like(ugrad_ref)

    tile = tile_ref[slot]

    @pl.when(tile < 0)
    def _():
        keep_ref[...] = jnp.zeros_like(keep_ref)
        send_ref[...] = jnp.zeros_like(send_ref)

    @pl.when(tile >= 0)
    def _():
        user_b = user_ref[...].astype(jnp.bfloat16)
        take = jnp.full(stale_ref.shape[1:], fresh_ref[slot], jnp.int32) == 1
        used = jnp.where(take, new_ref[0], stale_ref[0])
        pred = lax.dot_general(user_b, used, (((1,), (1,)), ((), ())), preferred_element_type=jnp.float32)
        marks = mark_ref[...]
        column = lax.broadcasted_iota(jnp.int32, marks.shape, 1)
        mark = jnp.sum(jnp.where(column == tile, marks, 0), axis=1, keepdims=True).astype(jnp.float32)
        err = (mark * (rate_ref[...].astype(jnp.float32) - pred)).astype(jnp.bfloat16)
        grad_ref[...] = lax.dot_general(err, user_b, (((0,), (0,)), ((), ())), preferred_element_type=jnp.float32)
        ugrad_ref[...] += jnp.dot(err, used, preferred_element_type=jnp.float32)
        core = core_ref[0]
        half = rows // 2
        keep_ref[0] = grad_ref[pl.ds(core * half, half), :].astype(jnp.bfloat16)
        send_ref[0] = grad_ref[pl.ds((1 - core) * half, half), :].astype(jnp.bfloat16)


def tiles(chunk, rows, block, scalars, users, marks, ratings, stale, fresh):
    slots = scalars[0].shape[0]
    n_users, width = users.shape
    per = block // rows

    def at(ref, i):
        return jnp.maximum(ref[i], 0)

    grid = pltpu.PrefetchScalarGridSpec(
        num_scalar_prefetch=4,
        grid=(slots,),
        in_specs=[
            pl.BlockSpec((n_users, width), lambda i, t, f, p, c: (0, 0)),
            pl.BlockSpec(marks.shape, lambda i, t, f, p, c: (0, 0)),
            pl.BlockSpec((n_users, rows), lambda i, t, f, p, c: (0, at(t, i) * per + chunk)),
            pl.BlockSpec((1, rows, width), lambda i, t, f, p, c: (at(t, i), chunk, 0)),
            pl.BlockSpec((1, rows, width), lambda i, t, f, p, c: (at(p, i), 0, 0)),
        ],
        out_specs=[
            pl.BlockSpec((1, rows // 2, width), lambda i, t, f, p, c: (i, 0, 0)),
            pl.BlockSpec((1, rows // 2, width), lambda i, t, f, p, c: (i, 0, 0)),
            pl.BlockSpec((n_users, width), lambda i, t, f, p, c: (0, 0)),
        ],
        scratch_shapes=[pltpu.VMEM((rows, width), jnp.float32)],
    )
    half = jax.ShapeDtypeStruct((slots, rows // 2, width), jnp.bfloat16)
    flops = 6 * slots * n_users * rows * width
    moved = 2 * slots * rows * (3 * width + n_users)
    return pl.pallas_call(
        functools.partial(tile_kernel, rows),
        grid_spec=grid,
        out_shape=(half, half, jax.ShapeDtypeStruct((n_users, width), jnp.float32)),
        compiler_params=pltpu.CompilerParams(vmem_limit_bytes=24 * 2**20),
        cost_estimate=pl.CostEstimate(flops=flops, bytes_accessed=moved, transcendentals=0),
    )(*scalars, users, marks, ratings, stale, fresh)


def swap(value, axis, bit):
    size = lax.axis_size(axis)
    return lax.ppermute(value, axis, [(i, i ^ (1 << bit)) for i in range(size)])


def my_bit(axis, bit):
    return (lax.axis_index(axis) >> bit) & 1


def spread(ids, value):
    out = []
    for j in range(BPS):
        hit = (ids == j)[..., None, None]
        out.append(jnp.sum(jnp.where(hit, value.astype(jnp.float32), 0.0), axis=-3, dtype=jnp.float32))
    return jnp.stack(out, axis=-3)


def steps_of(order, work_bits, serv_bits):
    out = []
    for name in order:
        if name == "w":
            out += [("work", b) for b in range(1, work_bits)]
        elif name == "s":
            out += [("serv", b) for b in range(min(1, serv_bits))]
        elif name == "z":
            out += [("serv", b) for b in range(1, serv_bits)]
        else:
            out += [("serv", b) for b in range(serv_bits - 1, 0, -1)]
    return out


def reduce_group(steps, ids, other_ids, kept, got, serv_bits):
    left = list(range(serv_bits - 1, -1, -1))
    lead = (2,) * serv_bits
    first = True
    kept, got = (v.reshape(lead + v.shape[1:]) for v in (kept, got))
    ids, other_ids = (v.reshape(lead + v.shape[1:]) for v in (ids, other_ids))
    for axis, bit in steps:
        here = my_bit(axis, bit)

        def part(value, which, has_rows=True):
            if axis == "serv":
                return lax.dynamic_index_in_dim(value, which, left.index(bit), keepdims=False)
            if not has_rows:
                return value
            dim = value.ndim - 2
            size = value.shape[dim] // 2
            return lax.dynamic_slice_in_dim(value, which * size, size, dim)

        def total(which):
            if first:
                return spread(part(ids, which, False), part(kept, which)) + spread(
                    part(other_ids, which, False), part(got, which)
                )
            return part(kept, which) + part(got, which).astype(jnp.float32)

        sent = swap(total(1 - here).astype(jnp.bfloat16), axis, bit)
        kept = total(here)
        got = sent
        if axis == "serv":
            left.remove(bit)
        first = False
    return kept + got.astype(jnp.float32)


def shards(user_factors, ratings, row_mask, touched, stale_cache, item_factors, roster):
    servers = lax.axis_size("serv")
    workers = lax.axis_size("work")
    work_bits = workers.bit_length() - 1
    serv_bits = servers.bit_length() - 1
    count = touched.shape[1]
    width = item_factors.shape[1]
    block = ratings.shape[1] // count
    rows = block // CHUNKS
    ids = touched[0]
    owners = ids // BPS
    order = jnp.arange(count, dtype=jnp.int32)
    same = (owners[:, None] == owners[None, :]) & (order[None, :] < order[:, None])
    slot = owners * CAP + jnp.sum(same.astype(jnp.int32), axis=1)
    slots_all = jnp.arange(servers * CAP, dtype=jnp.int32)
    placing = slot[None, :] == slots_all[:, None]
    tile = jnp.sum(jnp.where(placing, order[None, :] + 1, 0), axis=1) - 1
    slot_ids = jnp.sum(jnp.where(placing, ids[None, :] + 1, 0), axis=1) - 1
    is_fresh = ((slots_all // CAP == roster[0]) & (tile >= 0)).astype(jnp.int32)
    local = jnp.where(tile >= 0, slot_ids % BPS, -1)
    pick = jnp.where(is_fresh == 1, local, 0)
    core = my_bit("work", 0).reshape(1).astype(jnp.int32)
    other = swap(local, "work", 0)
    local = local.reshape(servers, CAP)
    other = other.reshape(servers, CAP)
    stale = stale_cache.reshape(count, block, width)
    mine = lax.axis_index("serv") == roster[0]
    items = item_factors.reshape(BPS, block, width)
    user_grad = 0.0
    pieces = []
    for chunk in range(CHUNKS):
        own = items[:, chunk * rows : (chunk + 1) * rows].astype(jnp.bfloat16)
        fresh = lax.psum(jnp.where(mine, own, jnp.zeros_like(own)), "serv")
        kept, send, ugrad = tiles(
            chunk, rows, block, (tile, is_fresh, pick, core), user_factors, row_mask, ratings, stale, fresh
        )
        user_grad = user_grad + ugrad
        half = rows // 2
        start = 0
        sums = []
        for share, route in GROUPS:
            size = half * share // 16
            cut = lambda v: v[:, start : start + size].reshape(servers, CAP, size, width)
            got = swap(send[:, start : start + size], "work", 0).reshape(servers, CAP, size, width)
            sums.append(
                reduce_group(steps_of(route, work_bits, serv_bits), local, other, cut(kept), got, serv_bits)
            )
            start += size
        mine_sum = jnp.concatenate(sums, axis=1).astype(jnp.bfloat16)
        whole = lax.all_gather(mine_sum, "work", axis=0)
        start = 0
        parts = []
        for share, _ in GROUPS:
            size = half * share // 16 // (workers // 2)
            part = whole[:, :, start : start + size].reshape((2,) * work_bits + (BPS, size, width))
            dims = (work_bits,) + tuple(range(work_bits - 1, -1, -1)) + (work_bits + 1, work_bits + 2)
            parts.append(part.transpose(dims).reshape(BPS, 2, half * share // 16, width))
            start += size
        pieces.append(jnp.concatenate(parts, axis=2).reshape(BPS, rows, width))
    users_next = user_factors - 0.05 * (0.1 * user_factors - user_grad)
    grad_sum = jnp.concatenate(pieces, axis=1).astype(jnp.float32)
    items_next = (items - 0.01 * (grad_sum + 0.1 * items)).reshape(BPS * block, width)
    return (users_next, items_next)


def solution(mesh):
    both = P(("work", "serv"), None)
    in_specs = (both, both, both, both, both, P("serv", None), P("work"))
    return jax.shard_map(shards, mesh=mesh, in_specs=in_specs, out_specs=(both, P("serv", None)), check_vma=False)
```

```python
import functools

import jax
import jax.numpy as jnp
from jax import lax
from jax.experimental import pallas as pl
from jax.experimental.pallas import tpu as pltpu
from jax.sharding import PartitionSpec as P

BPS = 4
CAP = 2
GROUPS = ((4, "wsz"), (4, "swz"), (4, "wsz"), (4, "swz"))
CAST_ROUTES = ("sz", "zs")
TILES_PER_CALL = 3


def tile_kernel(rows, slot_ref, tile_ref, source_ref, core_ref, user_ref, mark_ref, rate_ref, used_ref, before_ref,
                keep_in, send_in, keep_ref, send_ref, ugrad_ref, grad_ref):
    step = pl.program_id(0)

    @pl.when(step == 0)
    def _():
        ugrad_ref[...] = before_ref[...]

    tile = tile_ref[step]

    @pl.when(tile < 0)
    def _():
        keep_ref[...] = jnp.zeros_like(keep_ref)
        send_ref[...] = jnp.zeros_like(send_ref)

    @pl.when(tile >= 0)
    def _():
        user_b = user_ref[...].astype(jnp.bfloat16)
        used = used_ref[0]
        pred = lax.dot_general(user_b, used, (((1,), (1,)), ((), ())), preferred_element_type=jnp.float32)
        marks = mark_ref[...]
        column = lax.broadcasted_iota(jnp.int32, marks.shape, 1)
        mark = jnp.sum(jnp.where(column == tile, marks, 0), axis=1, keepdims=True).astype(jnp.float32)
        err = (mark * (rate_ref[...].astype(jnp.float32) - pred)).astype(jnp.bfloat16)
        grad_ref[...] = lax.dot_general(err, user_b, (((0,), (0,)), ((), ())), preferred_element_type=jnp.float32)
        ugrad_ref[...] += jnp.dot(err, used, preferred_element_type=jnp.float32)
        core = core_ref[0]
        half = rows // 2
        keep_ref[0] = grad_ref[pl.ds(core * half, half), :].astype(jnp.bfloat16)
        send_ref[0] = grad_ref[pl.ds((1 - core) * half, half), :].astype(jnp.bfloat16)


def tiles(scalars, users, marks, ratings, source, ugrad, keep, send):
    n = scalars[0].shape[0]
    n_users, width = users.shape
    rows = source.shape[1]

    def at(ref, i):
        return jnp.maximum(ref[i], 0)

    out_block = pl.BlockSpec((1, rows // 2, width), lambda i, s, t, f, c: (s[i], 0, 0))
    whole = pl.BlockSpec((n_users, width), lambda i, s, t, f, c: (0, 0))
    grid = pltpu.PrefetchScalarGridSpec(
        num_scalar_prefetch=4,
        grid=(n,),
        in_specs=[
            whole,
            pl.BlockSpec(marks.shape, lambda i, s, t, f, c: (0, 0)),
            pl.BlockSpec((n_users, rows), lambda i, s, t, f, c: (0, at(t, i))),
            pl.BlockSpec((1, rows, width), lambda i, s, t, f, c: (at(f, i), 0, 0)),
            whole,
            pl.BlockSpec(memory_space=pl.ANY),
            pl.BlockSpec(memory_space=pl.ANY),
        ],
        out_specs=[out_block, out_block, whole],
        scratch_shapes=[pltpu.VMEM((rows, width), jnp.float32)],
    )
    half = jax.ShapeDtypeStruct(keep.shape, jnp.bfloat16)
    flops = 6 * n * n_users * rows * width
    moved = 2 * n * rows * (3 * width + n_users) + 12 * n_users * width
    return pl.pallas_call(
        functools.partial(tile_kernel, rows),
        grid_spec=grid,
        out_shape=(half, half, jax.ShapeDtypeStruct((n_users, width), jnp.float32)),
        input_output_aliases={9: 0, 10: 1},
        compiler_params=pltpu.CompilerParams(vmem_limit_bytes=56 * 2**20),
        cost_estimate=pl.CostEstimate(flops=flops, bytes_accessed=moved, transcendentals=0),
    )(*scalars, users, marks, ratings, source, ugrad, keep, send)


def swap(value, axis, bit):
    size = lax.axis_size(axis)
    return lax.ppermute(value, axis, [(i, i ^ (1 << bit)) for i in range(size)])


def my_bit(axis, bit):
    return (lax.axis_index(axis) >> bit) & 1


def spread(ids, value):
    out = []
    for j in range(BPS):
        hit = (ids == j)[..., None, None]
        out.append(jnp.sum(jnp.where(hit, value.astype(jnp.float32), 0.0), axis=-3, dtype=jnp.float32))
    return jnp.stack(out, axis=-3)


def steps_of(order, work_bits, serv_bits):
    out = []
    for name in order:
        if name == "w":
            out += [("work", b) for b in range(1, work_bits)]
        elif name == "s":
            out += [("serv", b) for b in range(min(1, serv_bits))]
        elif name == "z":
            out += [("serv", b) for b in range(1, serv_bits)]
        else:
            out += [("serv", b) for b in range(serv_bits - 1, 0, -1)]
    return out


def reduce_group(steps, ids, other_ids, kept, got, serv_bits):
    left = list(range(serv_bits - 1, -1, -1))
    lead = (2,) * serv_bits
    first = True
    kept, got = (v.reshape(lead + v.shape[1:]) for v in (kept, got))
    ids, other_ids = (v.reshape(lead + v.shape[1:]) for v in (ids, other_ids))
    for axis, bit in steps:
        here = my_bit(axis, bit)

        def part(value, which, has_rows=True):
            if axis == "serv":
                return lax.dynamic_index_in_dim(value, which, left.index(bit), keepdims=False)
            if not has_rows:
                return value
            dim = value.ndim - 2
            size = value.shape[dim] // 2
            return lax.dynamic_slice_in_dim(value, which * size, size, dim)

        def total(which):
            if first:
                return spread(part(ids, which, False), part(kept, which)) + spread(
                    part(other_ids, which, False), part(got, which)
                )
            return part(kept, which) + part(got, which).astype(jnp.float32)

        sent = swap(total(1 - here).astype(jnp.bfloat16), axis, bit)
        kept = total(here)
        got = sent
        if axis == "serv":
            left.remove(bit)
        first = False
    return kept + got.astype(jnp.float32)


def cast_step(root, value, bits, step):
    if step < len(bits):
        bit = bits[step]
        here = my_bit("serv", bit)
        size = value.shape[1] // 2
        got = swap(lax.dynamic_slice_in_dim(value, (1 - here) * size, size, 1), "serv", bit)
        own = lax.dynamic_slice_in_dim(value, here * size, size, 1)
        return jnp.where(((root >> bit) & 1) == here, own, got)
    bit = bits[2 * len(bits) - 1 - step]
    low = my_bit("serv", bit) == 0
    got = swap(value, "serv", bit)
    return jnp.concatenate([jnp.where(low, value, got), jnp.where(low, got, value)], axis=1)


def shards(user_factors, ratings, row_mask, touched, stale_cache, item_factors, roster):
    servers = lax.axis_size("serv")
    workers = lax.axis_size("work")
    work_bits = workers.bit_length() - 1
    serv_bits = servers.bit_length() - 1
    count = touched.shape[1]
    width = item_factors.shape[1]
    block = ratings.shape[1] // count
    ids = touched[0]
    owners = ids // BPS
    order = jnp.arange(count, dtype=jnp.int32)
    same = (owners[:, None] == owners[None, :]) & (order[None, :] < order[:, None])
    slot = owners * CAP + jnp.sum(same.astype(jnp.int32), axis=1)
    slots_all = jnp.arange(servers * CAP, dtype=jnp.int32)
    placing = slot[None, :] == slots_all[:, None]
    tile = jnp.sum(jnp.where(placing, order[None, :] + 1, 0), axis=1) - 1
    slot_ids = jnp.sum(jnp.where(placing, ids[None, :] + 1, 0), axis=1) - 1
    local = jnp.where(tile >= 0, slot_ids % BPS, -1)
    core = my_bit("work", 0).reshape(1).astype(jnp.int32)
    other = swap(local, "work", 0).reshape(servers, CAP)
    root = roster[0]
    stale = stale_cache.reshape(count, block, width)
    items = item_factors.reshape(BPS, block, width)
    items_b = items.astype(jnp.bfloat16)
    share = block // len(CAST_ROUTES)
    cast = [items_b[:, i * share : (i + 1) * share] for i in range(len(CAST_ROUTES))]
    bits = [[b for _, b in steps_of(r, work_bits, serv_bits)] for r in CAST_ROUTES]
    kept = jnp.zeros((servers * CAP, block // 2, width), jnp.bfloat16)
    send = jnp.zeros_like(kept)
    user_grad = jnp.zeros(user_factors.shape, jnp.float32)
    rest = (servers - 1) * CAP
    starts = list(range(0, rest, TILES_PER_CALL))
    for step in range(max(2 * serv_bits, len(starts))):
        if step < 2 * serv_bits:
            cast = [cast_step(root, v, b, step) for v, b in zip(cast, bits)]
        if step < len(starts):
            start = starts[step]
            places = jnp.arange(start, min(start + TILES_PER_CALL, rest), dtype=jnp.int32)
            places = places + jnp.where(places >= root * CAP, CAP, 0)
            these = jnp.take(tile, places)
            kept, send, user_grad = tiles(
                (places, these, these, core), user_factors, row_mask, ratings, stale, user_grad, kept, send
            )
            cast, user_grad = lax.optimization_barrier((cast, user_grad))
    fresh = jnp.concatenate(cast, axis=1)
    places = root * CAP + jnp.arange(CAP, dtype=jnp.int32)
    scalars = (places, jnp.take(tile, places), jnp.take(local, places), core)
    kept, send, user_grad = tiles(scalars, user_factors, row_mask, ratings, fresh, user_grad, kept, send)
    local = local.reshape(servers, CAP)
    half = block // 2
    start = 0
    sums = []
    for part, route in GROUPS:
        size = half * part // 16
        got = swap(send[:, start : start + size], "work", 0).reshape(servers, CAP, size, width)
        mine = kept[:, start : start + size].reshape(servers, CAP, size, width)
        sums.append(reduce_group(steps_of(route, work_bits, serv_bits), local, other, mine, got, serv_bits))
        start += size
    mine_sum = jnp.concatenate(sums, axis=1).astype(jnp.bfloat16)
    whole = lax.all_gather(mine_sum, "work", axis=0)
    start = 0
    parts = []
    for part, _ in GROUPS:
        size = half * part // 16 // (workers // 2)
        piece = whole[:, :, start : start + size].reshape((2,) * work_bits + (BPS, size, width))
        dims = (work_bits,) + tuple(range(work_bits - 1, -1, -1)) + (work_bits + 1, work_bits + 2)
        parts.append(piece.transpose(dims).reshape(BPS, 2, half * part // 16, width))
        start += size
    grad_sum = jnp.concatenate(parts, axis=2).reshape(BPS, block, width).astype(jnp.float32)
    users_next = user_factors - 0.05 * (0.1 * user_factors - user_grad)
    items_next = (items - 0.01 * (grad_sum + 0.1 * items)).reshape(BPS * block, width)
    return (users_next, items_next)


def solution(mesh):
    both = P(("work", "serv"), None)
    in_specs = (both, both, both, both, both, P("serv", None), P("work"))
    return jax.shard_map(shards, mesh=mesh, in_specs=in_specs, out_specs=(both, P("serv", None)), check_vma=False)
```
